256 devices in a mesh: dp: 16 (over x, y_lo, core), section: 8 (over z), mp: 2 (over y_hi).
Axes of the slice: x: 4, y: 4 (y_hi: 2, y_lo: 2; y = y_hi * 2 + y_lo), z: 8, core: 2. Of those that a mesh axis runs over, the one named last changes fastest.
Arguments:
- enc_states: bfloat16 [8192, 4096], P('dp', ('section', 'mp')), may hold values from -0.0625 to 0.0625
- value_weight: bfloat16 [8, 4096, 2048], P('section', None, 'mp'), may hold values from -0.09375 to 0.09375
- attn_weights: bfloat16 [8, 8, 4096, 512], P('section', 'mp', 'dp'), may hold values from 0 to 1
- ctx_grad: bfloat16 [8, 4096, 2048], P('section', 'dp', 'mp'), may hold values from -0.1796875 to 0.1796875
- prompt_lengths: int32 [16], P('dp'), may hold values from 128 to 512, as said below
Outputs:
- enc_grad: bfloat16 [8192, 4096], P('dp', ('section', 'mp'))
- value_grad: float32 [8, 4096, 2048], P('section', 'dp', 'mp')
The draws below stay inside these ranges and needn't reach their ends.
Inputs may be any that keep to these rules, and one draw needn't show every extreme that they name: `prompt_lengths`: at least one sequence has the full length 512.
All inputs are finite; a program needn't handle non-finite values.
Results may differ from the reference program's by a relative error of at most 0.005.
Values may be sent and summed in bfloat16 or wider, within the bound.
A program may use at most 128 MiB of HBM per device.

```python
import jax
import jax.numpy as jnp
from jax import lax

D = 4096
HEADS = 8
HEAD_DIM = 256
ENC_DEV = 512
DEC_DEV = 256
WIDTH = 2048
LAYERS = 8
SEQS = 16
TOK_ENC = 8192
TOK_DEC = 4096


def draw_prompt_lengths(key, part):
    key = jax.random.fold_in(key, 7)
    first_key, second_key = jax.random.split(key)
    drawn = jax.random.randint(first_key, (SEQS,), ENC_DEV // 4, ENC_DEV + 1)
    chosen = jax.random.randint(second_key, (), 0, SEQS)
    return jnp.where(jnp.arange(SEQS) == chosen, ENC_DEV, drawn).astype(jnp.int32)


def shard_levels(rng, dims, shards, smallest, largest):
    loudness = 1.0
    for axis_at, shards_of in shards:
        draws = jax.random.uniform(jax.random.fold_in(jax.random.fold_in(rng, 6), axis_at), (shards_of,), jnp.float32, smallest / len(shards), largest / len(shards))
        loudness = loudness * jnp.repeat(jnp.exp(draws), dims[axis_at] // shards_of).reshape((-1,) + (1,) * (len(dims) - 1 - axis_at))
    return loudness


def noise(rng, shape, width, reach, pieces=(), kind=jnp.bfloat16):
    entries = jax.random.normal(rng, shape, jnp.float32) * width
    if len(pieces) > 0:
        entries = shard_levels(rng, shape, pieces, -0.22, 0.18) * entries
    return jnp.clip(entries, min=-reach, max=reach).astype(kind)


def setup_inputs(seed: int = 0) -> dict:
    streams_of = jax.random.split(jax.random.key(seed), 6)
    return {
        "enc_states": noise(streams_of[0], (TOK_ENC, D), TOK_ENC ** -0.5, 0.0625, ((0, 16), (1, 16))),
        "value_weight": noise(streams_of[1], (LAYERS, D, WIDTH), D ** -0.5, 0.09375, ((0, 8), (2, 2))),
        "attn_weights": jnp.clip(1.0 * jax.random.uniform(streams_of[2], (LAYERS, HEADS, TOK_DEC, ENC_DEV), jnp.float32) ** shard_levels(streams_of[2], (LAYERS, HEADS, TOK_DEC, ENC_DEV), ((0, 8), (1, 2), (2, 16)), -0.2, 0.2), 0.0, 1.0).astype(jnp.bfloat16),
        "ctx_grad": noise(streams_of[3], (LAYERS, TOK_DEC, WIDTH), 0.03, 0.1796875, ((0, 8), (1, 16), (2, 2))),
        "prompt_lengths": draw_prompt_lengths(jax.random.fold_in(streams_of[5], 71), 0),
    }


def reference(enc_states, value_weight, attn_weights, ctx_grad, prompt_lengths):
    positions = jnp.arange(ENC_DEV, dtype=jnp.int32)
    keeping = (positions[None, :] < prompt_lengths[:, None]).astype(jnp.float32)

    def one_layer(running, inputs):
        weight, probs, grads_ctx = inputs
        probs_four = probs.astype(jnp.float32).reshape(HEADS, SEQS, DEC_DEV, ENC_DEV)
        grads_four = grads_ctx.astype(jnp.float32).reshape(SEQS, DEC_DEV, HEADS, HEAD_DIM)
        values_raw = jnp.einsum("hsqe,sqhd->sehd", probs_four, grads_four).reshape(SEQS, ENC_DEV, WIDTH)
        value_grads = (values_raw * keeping[:, :, None]).astype(jnp.bfloat16).reshape(TOK_ENC, WIDTH)
        partial_enc = jnp.dot(value_grads, weight.T, preferred_element_type=jnp.float32)
        weight_grad = jnp.dot(enc_states.T, value_grads, preferred_element_type=jnp.float32)
        return running + partial_enc, weight_grad

    start_sum = jnp.zeros((TOK_ENC, D), jnp.float32)
    summed, weight_grads = lax.scan(one_layer, start_sum, (value_weight, attn_weights, ctx_grad))
    return summed.astype(jnp.bfloat16), weight_grads
```

```python
import jax
import jax.numpy as jnp
from jax import lax
from jax.experimental import pallas as pl
from jax.experimental.pallas import tpu as pltpu
from jax.sharding import PartitionSpec as P


MESH = pl.DeviceIdType.MESH
REL = (4, 3, 5, 2, 6, 1, 7, 0)
POS = {rel: slot for slot, rel in enumerate(REL)}
BF16 = jnp.bfloat16
F32 = jnp.float32


def dot(a, b, ca, cb):
    return lax.dot_general(a, b, (((ca,), (cb,)), ((), ())), preferred_element_type=F32)


def kernel(
    lens, enc, weight, attn, ctx, eg_out, vg_out,
    attn_v, ctx_v, ebuf, et, val, wq, zsum, zs, zr, gkeep, gs, gr, xs, xr, fs, fr,
    lsem, wlsem, essem, ersem, vssem, vrsem, wssem, wrsem, zssem, zrsem,
    gssem, grsem, xssem, xrsem, fssem, frsem, ossem, orsem,
):
    dp, z, m = lax.axis_index("dp"), lax.axis_index("section"), lax.axis_index("mp")
    x, s, c = dp // 4, (dp // 2) % 2, dp % 2

    def dev(x_, s_, c_, z_, m_):
        return (x_ * 4 + s_ * 2 + c_, z_, m_)

    n1 = dev(x, 1 - s, c, z, m)
    n2 = dev(x, 1 - s, c, z, 1 - m)
    peer = dev(x, s, 1 - c, z, m)
    zdev = (dev(x, s, c, (z + 1) % 8, m), dev(x, s, c, (z + 7) % 8, m))
    xdev = tuple(dev((x + k) % 4, s, c, z, m) for k in (1, 2, 3))
    selfy = jnp.logical_and(s == c, c == m)
    same = selfy.astype(jnp.int32)
    sends = []

    def remote(src, dst, ss, rs, where):
        return pltpu.make_async_remote_copy(
            src_ref=src, dst_ref=dst, send_sem=ss, recv_sem=rs, device_id=where, device_id_type=MESH
        )

    def go(copy):
        copy.start()
        sends.append(copy)

    own_enc = pltpu.make_async_copy(
        enc.at[:, pl.ds(pl.multiple_of(s * 128, 128), 128)], ebuf.at[0, 0], lsem.at[0]
    )
    own_attn = pltpu.make_async_copy(attn.at[0], attn_v, lsem.at[1])
    own_ctx = pltpu.make_async_copy(ctx.at[0], ctx_v, lsem.at[2])
    own_enc.start()
    own_ctx.start()
    own_attn.start()

    def weight_rows(slot_rel, m_, s_):
        layer = (z + slot_rel) % 8
        return pl.ds(pl.multiple_of((2 * layer + m_) * 256 + s_ * 128, 128), 128)

    own_w = []
    for slot in range(8):
        own_w.append(
            pltpu.make_async_copy(
                weight.at[0, weight_rows(REL[slot], m, s), :], wq.at[0, pl.ds(slot * 128, 128), :], wlsem.at[slot]
            )
        )

    barrier = pltpu.get_barrier_semaphore()
    for where in (n1, n2, peer) + zdev + xdev:
        pl.semaphore_signal(barrier, inc=1, device_id=where, device_id_type=MESH)
    for half in range(2):
        @pl.when(jnp.logical_not(jnp.logical_and(selfy, s == half)))
        def _():
            pl.semaphore_signal(barrier, inc=1, device_id=dev(x, half, s, z, c), device_id_type=MESH)
    pl.semaphore_wait(barrier, 10 - same)

    pre = remote(
        enc.at[:, pl.ds(pl.multiple_of((1 - s) * 128, 128), 128)], ebuf.at[1, 0], essem.at[1, 0], ersem.at[1, 0], n1
    )
    go(pre)
    own_enc.wait()

    ecopy = {}
    for part in range(2):
        for direction in range(2):
            for step in range(4 if part == direction else 3):
                src = (8 - step) % 8 if direction else step
                to = 7 - step if direction else step + 1
                ecopy[part, to] = remote(
                    ebuf.at[part, src], ebuf.at[part, to], essem.at[part, to], ersem.at[part, to], zdev[direction]
                )
    go(ecopy[0, 1])
    go(ecopy[0, 7])

    piece = 2 * x + c
    piece_rel = 0
    for slot in range(8):
        piece_rel = jnp.where(piece == slot, REL[slot], piece_rel)
    piece_rows = pl.ds(pl.multiple_of(piece * 128, 128), 128)
    w_in = remote(
        weight.at[0, weight_rows(piece_rel, 1 - m, 1 - s), :], wq.at[1, piece_rows, :], wssem.at[0], wrsem.at[0], n2
    )
    go(w_in)
    for copy in own_w:
        copy.start()

    own_ctx.wait()
    own_attn.wait()
    keep = (lax.broadcasted_iota(jnp.int32, (512, 256), 0) < lens[0]).astype(F32)
    vcopy = {}
    for h in range(4):
        vcopy[1, h] = remote(val.at[0, h], val.at[1, h], vssem.at[1, h], vrsem.at[1, h], n1)
        vcopy[3, h] = remote(val.at[0, h], val.at[3, h], vssem.at[3, h], vrsem.at[3, h], n2)
        if h < 2:
            vcopy[2, h] = remote(val.at[3, h], val.at[2, h], vssem.at[2, h], vrsem.at[2, h], n1)
        else:
            vcopy[2, h] = remote(val.at[1, h], val.at[2, h], vssem.at[2, h], vrsem.at[2, h], n2)
        raw = dot(attn_v[h], ctx_v[:, h * 256 : (h + 1) * 256], 0, 0)
        val[0, h] = (raw * keep).astype(BF16)
        go(vcopy[1, h])
        go(vcopy[3, h])

    def put_et(part, rel):
        layer = (z + 8 - rel) % 8
        row = ((layer + c) % 2 * 4 + (layer // 2 + 4 - x) % 4) * 128
        et[part, pl.ds(pl.multiple_of(row, 128), 128), :] = ebuf[part, rel].T

    def enc_in(part, rel):
        ecopy[part, rel].wait_recv()
        following = rel - 1 if rel > 4 or (rel == 4 and part == 1) else rel + 1
        if (part, following) in ecopy and 0 < following < 8:
            up = rel < 4 or (rel == 4 and part == 0)
            if (up and following <= (4 if part == 0 else 3)) or (not up and following >= (5 if part == 0 else 4)):
                go(ecopy[part, following])
        put_et(part, rel)

    def value_in(h):
        vcopy[3, h].wait_recv()
        if h < 2:
            go(vcopy[2, h])
        vcopy[1, h].wait_recv()
        if h >= 2:
            go(vcopy[2, h])

    def z_part(part, pair, which, first):
        slot = {(0, 0): 0, (0, 1): 2, (1, 0): 1, (1, 1): 3}[part, which]
        rows = wq.at[which, pl.ds(pair * 256, 256), :]
        acc = None
        for h in range(4):
            term = dot(val[slot, h], rows[:, h * 256 : (h + 1) * 256], 1, 1)
            acc = term if acc is None else acc + term
        for i in range(2):
            half = acc[:, i * 128 : (i + 1) * 128]
            if first:
                zsum[part, 2 * pair + i] = half
            else:
                zsum[part, 2 * pair + i] += half

    put_et(0, 0)
    pre.wait_recv()
    go(ecopy[1, 1])
    go(ecopy[1, 7])
    put_et(1, 0)
    enc_in(0, 1)
    enc_in(0, 7)
    for copy in own_w:
        copy.wait()
    for pair in range(4):
        z_part(0, pair, 0, True)
    enc_in(1, 1)
    enc_in(1, 7)

    w_in.wait_recv()
    piece_ref = wq.at[1, piece_rows, :]
    w_x = [remote(piece_ref, piece_ref, wssem.at[1 + k], wrsem.at[1 + k], xdev[k]) for k in range(3)]
    w_c = []
    for k in range(4):
        there = (x + 4 - k) % 4
        ref = wq.at[1, pl.ds(pl.multiple_of((2 * there + c) * 128, 128), 128), :]
        w_c.append(remote(ref, ref, wssem.at[4 + k], wrsem.at[4 + k], peer))
    for copy in w_x:
        go(copy)
    go(w_c[0])
    value_in(0)
    enc_in(0, 2)
    enc_in(0, 6)
    enc_in(1, 2)
    enc_in(1, 6)
    value_in(1)
    enc_in(0, 3)
    enc_in(0, 5)
    value_in(2)
    enc_in(1, 3)
    enc_in(1, 5)
    for k in (0, 2, 1):
        w_x[k].wait_recv()
        go(w_c[k + 1])
    enc_in(0, 4)
    enc_in(1, 4)
    for k in range(4):
        w_c[k].wait_recv()
    value_in(3)

    STREAMS = ((0, 0), (0, 1), (1, 1), (1, 0))
    zcopy = {}
    for part in range(2):
        for direction, half in STREAMS:
            for step in range(4 if direction == half else 3):
                zcopy[part, direction, half, step] = remote(
                    zs.at[part, direction, half, step], zr.at[part, direction, half, step],
                    zssem.at[part, direction, half, step], zrsem.at[part, direction, half, step], zdev[direction],
                )

    def z_step(part, direction, half, step):
        length = 4 if direction == half else 3
        if step >= length:
            return
        ahead = length - step
        slot = POS[(8 - ahead) % 8 if direction else ahead]
        value = zsum[part, slot, half * 256 : (half + 1) * 256, :]
        if step > 0:
            zcopy[part, direction, half, step - 1].wait_recv()
            value = value + zr[part, direction, half, step - 1].astype(F32)
        zs[part, direction, half, step] = value.astype(BF16)
        go(zcopy[part, direction, half, step])

    def z_all(part, step):
        for direction, half in STREAMS:
            z_step(part, direction, half, step)

    col_mine = pl.ds(pl.multiple_of(s * 128, 128), 128)

    gcopy = [remote(gs.at[i], gr.at[i], gssem.at[i], grsem.at[i], peer) for i in range(8)]

    def g_head(f, h):
        i = f * 4 + h
        va, vb = (0, 1) if f == 0 else (2, 3)
        gs[i] = (dot(et[0, 512:, :], val[va, h], 1, 0) + dot(et[1, 512:, :], val[vb, h], 1, 0)).astype(BF16)
        go(gcopy[i])
        gkeep[i] = dot(et[0, :512, :], val[va, h], 1, 0) + dot(et[1, :512, :], val[vb, h], 1, 0)

    xcopy = {}
    for q in range(4):
        for k in range(3):
            xcopy[q, k] = remote(xs.at[q, k], xr.at[q, k], xssem.at[q, k], xrsem.at[q, k], xdev[k])

    def x_send(f, p):
        q = f * 2 + p
        for j in range(2):
            gcopy[f * 4 + p + 2 * j].wait_recv()
        for k in (1, 0, 2):
            for j in range(2):
                i = f * 4 + p + 2 * j
                rows = slice((k + 1) * 128, (k + 2) * 128)
                xs[q, k, j] = (gkeep[i, rows, :] + gr[i, rows, :].astype(F32)).astype(BF16)
            go(xcopy[q, k])

    fcopy = {}
    for q in range(4):
        fcopy[q] = remote(
            fs.at[q], fr.at[s, q % 2], fssem.at[q], frsem.at[s, q % 2], dev(x, c, m, z, m if q < 2 else 1 - m)
        )

    def f_send(f, p):
        q = f * 2 + p
        for k in range(3):
            xcopy[q, k].wait_recv()
        for j in range(2):
            i = f * 4 + p + 2 * j
            value = gkeep[i, :128, :] + gr[i, :128, :].astype(F32)
            for k in range(3):
                value = value + xr[q, k, j].astype(F32)
            fs[q, j] = value.astype(BF16)
        if f == 0:
            @pl.when(selfy)
            def _():
                fr[s, p] = fs[q]

            @pl.when(jnp.logical_not(selfy))
            def _():
                fcopy[q].start()
        else:
            go(fcopy[q])

    for pair in range(4):
        z_part(1, pair, 0, True)
        z_part(1, pair, 1, False)
        if pair == 0:
            z_step(1, 0, 0, 0)
            z_step(1, 1, 1, 0)
            z_step(1, 0, 1, 0)
        if pair == 1:
            z_step(1, 1, 0, 0)
    g_head(0, 0)
    g_head(0, 2)
    z_all(1, 1)
    x_send(0, 0)
    g_head(0, 1)
    g_head(0, 3)
    z_all(1, 2)
    x_send(0, 1)
    z_all(1, 3)
    vcopy[2, 0].wait_recv()
    g_head(1, 0)
    vcopy[2, 2].wait_recv()
    g_head(1, 2)
    x_send(1, 0)
    f_send(0, 0)
    vcopy[2, 1].wait_recv()
    vcopy[2, 3].wait_recv()
    for pair in range(4):
        z_part(0, pair, 1, False)
        if pair == 0:
            z_step(0, 0, 0, 0)
            z_step(0, 1, 1, 0)
            z_step(0, 0, 1, 0)
        if pair == 1:
            z_step(0, 1, 0, 0)
    g_head(1, 1)
    g_head(1, 3)
    z_all(0, 1)
    x_send(1, 1)
    for half in range(2):
        rows = slice(half * 256, (half + 1) * 256)
        value = zsum[1, POS[0], rows, :]
        for direction in range(2):
            step = (4 if direction == half else 3) - 1
            zcopy[1, direction, half, step].wait_recv()
            value = value + zr[1, direction, half, step].astype(F32)
        et[0, half * 256 : (half + 1) * 256, :128] = value.astype(BF16)
    out_copy = remote(et.at[0, pl.ds(0, 512), pl.ds(0, 128)], eg_out.at[:, col_mine], ossem.at[0], orsem.at[0], n1)
    go(out_copy)
    z_all(0, 2)
    f_send(0, 1)
    z_all(0, 3)
    f_send(1, 0)
    for half in range(2):
        rows = slice(half * 256, (half + 1) * 256)
        value = zsum[0, POS[0], rows, :]
        for direction in range(2):
            step = (4 if direction == half else 3) - 1
            zcopy[0, direction, half, step].wait_recv()
            value = value + zr[0, direction, half, step].astype(F32)
        eg_out[rows, col_mine] = value.astype(BF16)
    f_send(1, 1)

    for p in range(2):
        for half in range(2):
            @pl.when(jnp.logical_not(jnp.logical_and(selfy, s == half)))
            def _():
                remote(fs.at[p], fr.at[half, p], fssem.at[p], frsem.at[half, p], n1).wait_recv()
            for j in range(2):
                h = p + 2 * j
                vg_out[0, half * 128 : (half + 1) * 128, h * 256 : (h + 1) * 256] = fr[half, p, j].astype(F32)
    out_copy.wait_recv()
    for copy in sends:
        copy.wait_send()
    for q in range(2):
        @pl.when(jnp.logical_not(selfy))
        def _():
            fcopy[q].wait_send()


def local(enc_states, value_weight, attn_weights, ctx_grad, prompt_lengths):
    anywhere = pl.BlockSpec(memory_space=pl.ANY)
    vmem = pl.BlockSpec(memory_space=pltpu.VMEM)
    dma = pltpu.SemaphoreType.DMA
    enc_grad, value_grad = pl.pallas_call(
        kernel,
        out_shape=(jax.ShapeDtypeStruct((512, 256), BF16), jax.ShapeDtypeStruct((1, 256, 1024), F32)),
        in_specs=[pl.BlockSpec(memory_space=pltpu.SMEM)] + [anywhere] * 4,
        out_specs=(vmem, vmem),
        scratch_shapes=[
            pltpu.VMEM((4, 256, 512), BF16),
            pltpu.VMEM((256, 1024), BF16),
            pltpu.VMEM((2, 8, 512, 128), BF16),
            pltpu.VMEM((2, 1024, 512), BF16),
            pltpu.VMEM((4, 4, 512, 256), BF16),
            pltpu.VMEM((2, 1024, 1024), BF16),
            pltpu.VMEM((2, 8, 512, 128), F32),
            pltpu.VMEM((2, 2, 2, 4, 256, 128), BF16),
            pltpu.VMEM((2, 2, 2, 4, 256, 128), BF16),
            pltpu.VMEM((8, 512, 256), F32),
            pltpu.VMEM((8, 512, 256), BF16),
            pltpu.VMEM((8, 512, 256), BF16),
            pltpu.VMEM((4, 3, 2, 128, 256), BF16),
            pltpu.VMEM((4, 3, 2, 128, 256), BF16),
            pltpu.VMEM((4, 2, 128, 256), BF16),
            pltpu.VMEM((2, 2, 2, 128, 256), BF16),
            dma((3,)), dma((8,)),
            dma((2, 8)), dma((2, 8)),
            dma((4, 4)), dma((4, 4)),
            dma((8,)), dma((8,)),
            dma((2, 2, 2, 4)), dma((2, 2, 2, 4)),
            dma((8,)), dma((8,)),
            dma((4, 3)), dma((4, 3)),
            dma((4,)), dma((2, 2)),
            dma((1,)), dma((1,)),
        ],
        compiler_params=pltpu.CompilerParams(
            collective_id=0, has_side_effects=True, vmem_limit_bytes=60 * 2**20
        ),
        cost_estimate=pl.CostEstimate(flops=9 * 10**9, bytes_accessed=12 * 2**20, transcendentals=0),
    )(prompt_lengths, enc_states, value_weight, attn_weights, ctx_grad)
    return enc_grad, value_grad


def solution(mesh):
    in_specs = (
        P("dp", ("section", "mp")),
        P("section", None, "mp"),
        P("section", "mp", "dp", None),
        P("section", "dp", "mp"),
        P("dp"),
    )
    out_specs = (P("dp", ("section", "mp")), P("section", "dp", "mp"))
    return jax.shard_map(local, mesh=mesh, in_specs=in_specs, out_specs=out_specs, check_vma=False)
```

```python
import jax
import jax.numpy as jnp
from jax import lax
from jax.experimental import pallas as pl
from jax.experimental.pallas import tpu as pltpu
from jax.sharding import PartitionSpec as P


MESH = pl.DeviceIdType.MESH
REL = (4, 3, 5, 2, 6, 1, 7, 0)
POS = {rel: slot for slot, rel in enumerate(REL)}
BF16 = jnp.bfloat16
F32 = jnp.float32
WINDOW = 3
ORDER = (
    ("v", 3, 1), ("second", 0), ("et", 0, 0), ("zf", 0, 0), ("e", 0, 1, 0), ("e", 0, 7, 0), ("zf", 0, 1), ("won", 0),
    ("v", 3, 2), ("v", 1, 3), ("second", 1), ("et", 1, 0), ("e", 0, 1, 1), ("e", 0, 7, 1), ("e", 1, 7, 0),
    ("e", 1, 1, 0), ("won", 1), ("v", 3, 3), ("v", 1, 4), ("e", 0, 6, 0), ("e", 0, 2, 0), ("e", 1, 1, 1),
    ("e", 1, 7, 1), ("v", 1, 5), ("v", 3, 4), ("wac", 1, 0), ("e", 0, 2, 1), ("e", 0, 6, 1), ("e", 1, 2, 0),
    ("e", 1, 6, 0), ("v", 1, 6), ("v", 3, 5), ("wac", 2, 0), ("wac", 0, 0), ("e", 0, 5, 0), ("e", 0, 3, 0),
    ("e", 1, 2, 1), ("zf", 1, 0), ("wac", 1, 1), ("v", 1, 7), ("v", 3, 6), ("e", 1, 6, 1), ("e", 0, 3, 1),
    ("e", 0, 5, 1), ("e", 1, 5, 0), ("e", 1, 3, 0), ("v", 1, 8), ("v", 3, 7), ("wac", 2, 1), ("wac", 0, 1),
    ("e", 0, 4, 0), ("wdone",), ("zs", 1, 0), ("e", 1, 3, 1), ("e", 1, 5, 1), ("v", 1, 9), ("v", 3, 8),
    ("e", 0, 4, 1), ("e", 1, 4, 0), ("v", 1, 10), ("v", 3, 9), ("z", 1, 1, 0, 1), ("z", 1, 0, 0, 1),
    ("z", 1, 0, 1, 1), ("z", 1, 1, 1, 1), ("e", 1, 4, 1), ("g", 0, 0), ("g", 0, 1), ("z", 1, 0, 0, 2),
    ("z", 1, 0, 1, 2), ("v", 3, 10), ("x", 0, 0), ("zf", 1, 1), ("v", 3, 11), ("x", 0, 1), ("v", 1, 11),
    ("z", 1, 1, 0, 2), ("z", 1, 1, 1, 2), ("g", 0, 3), ("zs", 1, 1), ("z", 1, 0, 0, 3), ("g", 0, 2), ("x", 0, 3),
    ("g", 1, 0), ("x", 0, 2), ("g", 1, 1), ("z", 1, 1, 3, 1), ("z", 1, 1, 2, 1), ("x", 1, 0), ("z", 1, 0, 2, 1),
    ("f", 0, 1), ("z", 1, 0, 3, 1), ("zs", 0, 0), ("z", 1, 1, 1, 3), ("f", 0, 0), ("g", 1, 2), ("z", 1, 1, 3, 2),
    ("zs", 0, 1), ("z", 1, 1, 2, 2), ("z", 1, 0, 3, 2), ("x", 1, 2), ("z", 1, 0, 2, 2), ("z", 0, 1, 0, 1),
    ("f", 0, 3), ("z", 0, 0, 0, 1), ("x", 1, 1), ("z", 0, 0, 1, 1), ("f", 0, 2), ("z", 0, 1, 1, 1), ("ze", 1, 0),
    ("g", 1, 3), ("z", 1, 1, 3, 3), ("z", 0, 1, 2, 1), ("z", 0, 0, 2, 1), ("z", 0, 0, 3, 1), ("z", 0, 1, 3, 1),
    ("f", 1, 0), ("x", 1, 3), ("z", 1, 0, 2, 3), ("z", 0, 1, 0, 2), ("z", 0, 0, 0, 2), ("z", 0, 1, 1, 2),
    ("z", 0, 0, 1, 2), ("f", 1, 2), ("z", 0, 0, 2, 2), ("z", 0, 1, 2, 2), ("fin", 0), ("z", 0, 0, 3, 2),
    ("z", 0, 1, 3, 2), ("ze", 1, 1), ("out",), ("z", 0, 0, 0, 3), ("f", 1, 1), ("z", 0, 1, 1, 3), ("fin", 2),
    ("z", 0, 0, 2, 3), ("z", 0, 1, 3, 3), ("f", 1, 3), ("ze", 0, 0), ("fin", 1), ("ze", 0, 1), ("fin", 3),
)


def dot(a, b, ca, cb):
    return lax.dot_general(a, b, (((ca,), (cb,)), ((), ())), preferred_element_type=F32)


def kernel(
    lens, enc, weight, attn, ctx, enc_out, val_out,
    attn_v, ctx_v, ebuf, et, val, wq, zsum, zs, zr, gkeep, gs, gr, xs, xr, fs, zout,
    lsem, wlsem, essem, ersem, vssem, vrsem, wssem, wrsem, zssem, zrsem,
    gssem, grsem, xssem, xrsem, fssem, frsem, ossem, orsem,
):
    dp, z, m = lax.axis_index("dp"), lax.axis_index("section"), lax.axis_index("mp")
    x, s, c = dp // 4, (dp // 2) % 2, dp % 2

    def dev(x_, s_, c_, z_, m_):
        return (x_ * 4 + s_ * 2 + c_, z_, m_)

    n1 = dev(x, 1 - s, c, z, m)
    n2 = dev(x, 1 - s, c, z, 1 - m)
    peer = dev(x, s, 1 - c, z, m)
    zdev = (dev(x, s, c, (z + 1) % 8, m), dev(x, s, c, (z + 7) % 8, m))
    xdev = tuple(dev((x + k) % 4, s, c, z, m) for k in (1, 2, 3))
    selfy = jnp.logical_and(s == c, c == m)
    same = selfy.astype(jnp.int32)
    sends = []

    def remote(src, dst, ss, rs, where):
        return pltpu.make_async_remote_copy(
            src_ref=src, dst_ref=dst, send_sem=ss, recv_sem=rs, device_id=where, device_id_type=MESH
        )

    def go(copy):
        copy.start()
        sends.append(copy)

    def sent(copy):
        copy.wait_send()
        sends[:] = [other for other in sends if other is not copy]

    own_enc = pltpu.make_async_copy(
        enc.at[:, pl.ds(pl.multiple_of(s * 128, 128), 128)], ebuf.at[0, 0], lsem.at[0]
    )
    own_ctx = pltpu.make_async_copy(ctx.at[0], ctx_v, lsem.at[1])
    own_attn = [pltpu.make_async_copy(attn.at[0, h], attn_v.at[h], lsem.at[2 + h]) for h in range(4)]
    own_enc.start()
    own_attn[0].start()
    own_ctx.start()
    for h in range(1, 4):
        own_attn[h].start()

    def weight_rows(slot_rel, m_, s_):
        layer = (z + slot_rel) % 8
        return pl.ds(pl.multiple_of((2 * layer + m_) * 256 + s_ * 128, 128), 128)

    own_w = []
    for slot in range(8):
        own_w.append(
            pltpu.make_async_copy(
                weight.at[0, weight_rows(REL[slot], m, s), :], wq.at[0, pl.ds(slot * 128, 128), :], wlsem.at[slot]
            )
        )

    barrier = pltpu.get_barrier_semaphore()
    for where in (n1, n2, peer) + zdev + xdev:
        pl.semaphore_signal(barrier, inc=1, device_id=where, device_id_type=MESH)
    for half in range(2):
        @pl.when(jnp.logical_not(jnp.logical_and(selfy, s == half)))
        def _():
            pl.semaphore_signal(barrier, inc=1, device_id=dev(x, half, s, z, c), device_id_type=MESH)
    pl.semaphore_wait(barrier, 10 - same)

    row_half = (pl.ds(0, 256), pl.ds(256, 256))
    pre = []
    for u in range(2):
        src = enc.at[row_half[u], pl.ds(pl.multiple_of((1 - s) * 128, 128), 128)]
        pre.append(remote(src, ebuf.at[1, 0, row_half[u], :], essem.at[1, 0, u], ersem.at[1, 0, u], n1))
        go(pre[u])
    own_enc.wait()

    ecopy = {}
    for part in range(2):
        for u in range(2):
            for direction in range(2):
                for step in range(4 if (part == u) == (direction == 0) else 3):
                    src = (8 - step) % 8 if direction else step
                    to = 7 - step if direction else step + 1
                    ecopy[part, to, u] = remote(
                        ebuf.at[part, src, row_half[u], :], ebuf.at[part, to, row_half[u], :],
                        essem.at[part, to, u], ersem.at[part, to, u], zdev[direction],
                    )
    for u in range(2):
        go(ecopy[0, 1, u])
        go(ecopy[0, 7, u])

    piece = 2 * x + c
    piece_rel = 0
    for slot in range(8):
        piece_rel = jnp.where(piece == slot, REL[slot], piece_rel)
    layer_rows = (2 * ((z + piece_rel) % 8) + 1 - m) * 256 + (1 - s) * 128

    def weight_piece(owner, j):
        return wq.at[1, pl.ds(pl.multiple_of(owner * 128 + j * 64, 64), 64), :]

    w_in = []
    for j in range(2):
        rows = pl.ds(pl.multiple_of(layer_rows + j * 64, 64), 64)
        w_in.append(remote(weight.at[0, rows, :], weight_piece(piece, j), wssem.at[0, j], wrsem.at[0, j], n2))
        go(w_in[j])
    for copy in own_w:
        copy.start()


    def value_copy(src, to, h, t, where):
        return remote(
            val.at[src, h, row_half[t], :], val.at[to, h, row_half[t], :],
            vssem.at[to, h, t], vrsem.at[to, h, t], where,
        )

    vcopy = {}
    for h in range(4):
        for t in range(2):
            vcopy[1, h, t] = value_copy(0, 1, h, t, n1)
            vcopy[3, h, t] = value_copy(0, 3, h, t, n2)
            vcopy[2, h, t] = value_copy(3, 2, h, t, n1) if t == 0 else value_copy(1, 2, h, t, n2)
    queues = {}
    for to, through in ((1, 0), (3, 1)):
        queues[to] = [(to, h, t) for t in range(2) for h in range(4)] + [(2, h, through) for h in range(4)]
    arrived = set()

    def value_in(*key):
        if key not in arrived:
            arrived.add(key)
            vcopy[key].wait_recv()

    def value_next(to, i):
        if i >= WINDOW:
            sent(vcopy[queues[to][i - WINDOW]])
        key = queues[to][i]
        if key[0] == 2:
            value_in(4 - to, key[1], key[2])
        go(vcopy[key])

    own_ctx.wait()
    keep = (lax.broadcasted_iota(jnp.int32, (512, 256), 0) < lens[0]).astype(F32)
    for h in range(4):
        own_attn[h].wait()
        raw = dot(attn_v[h], ctx_v[:, h * 256 : (h + 1) * 256], 0, 0)
        val[0, h] = (raw * keep).astype(BF16)
        if h < WINDOW:
            value_next(1, h)
        if h == 0:
            value_next(3, 0)

    def put_et(part, rel, u):
        layer = (z + 8 - rel) % 8
        row = ((layer + c) % 2 * 4 + (layer // 2 + 4 - x) % 4) * 128
        columns = slice(u * 256, (u + 1) * 256)
        et[part, pl.ds(pl.multiple_of(row, 128), 128), columns] = ebuf[part, rel, columns, :].T

    def enc_first(part, rel):
        for u in range(2):
            put_et(part, rel, u)

    def enc_second(u):
        pre[u].wait_recv()
        go(ecopy[1, 1, u])
        go(ecopy[1, 7, u])

    def enc_in(part, rel, u):
        ecopy[part, rel, u].wait_recv()
        top = 4 if part == u else 3
        if rel < top:
            go(ecopy[part, rel + 1, u])
        elif rel > top + 1:
            go(ecopy[part, rel - 1, u])
        put_et(part, rel, u)

    def z_part(part, t, pair, which):
        slot = {(0, 0): 0, (0, 1): 2, (1, 0): 1, (1, 1): 3}[part, which]
        rows = wq.at[which, pl.ds(pair * 256, 256), :]
        acc = None
        for h in range(4):
            term = dot(val[slot, h, t * 256 : (t + 1) * 256, :], rows[:, h * 256 : (h + 1) * 256], 1, 1)
            acc = term if acc is None else acc + term
        for i in range(2):
            half = acc[:, i * 128 : (i + 1) * 128]
            if which == 0:
                zsum[part, 2 * pair + i, t * 256 : (t + 1) * 256, :] = half
            else:
                zsum[part, 2 * pair + i, t * 256 : (t + 1) * 256, :] += half

    own_w_waits = list(own_w)

    def z_first(part, t):
        while own_w_waits:
            own_w_waits.pop().wait()
        for h in range(4):
            if part == 1:
                value_in(1, h, t)
        for pair in range(4):
            z_part(part, t, pair, 0)

    w_x, w_c = {}, {}
    for j in range(2):
        for k in range(3):
            ref = weight_piece(piece, j)
            w_x[k, j] = remote(ref, ref, wssem.at[1 + k, j], wrsem.at[1 + k, j], xdev[k])
        for k in range(4):
            ref = weight_piece(2 * ((x + 4 - k) % 4) + c, j)
            w_c[k, j] = remote(ref, ref, wssem.at[4 + k, j], wrsem.at[4 + k, j], peer)

    def weight_on(j):
        w_in[j].wait_recv()
        for k in (1, 0, 2):
            go(w_x[k, j])
        go(w_c[0, j])

    def weight_across(k, j):
        w_x[k, j].wait_recv()
        go(w_c[k + 1, j])

    zcopy = {}
    for part in range(2):
        for direction in range(2):
            for tau in range(4):
                for step in range(4 if direction == tau % 2 else 3):
                    zcopy[part, direction, tau, step] = remote(
                        zs.at[part, direction, tau, step], zr.at[part, direction, tau, step],
                        zssem.at[part, direction, tau, step], zrsem.at[part, direction, tau, step], zdev[direction],
                    )

    def z_step(part, direction, tau, step):
        length = 4 if direction == tau % 2 else 3
        if step >= length:
            return
        ahead = length - step
        slot = POS[(8 - ahead) % 8 if direction else ahead]
        value = zsum[part, slot, tau * 128 : (tau + 1) * 128, :]
        if step > 0:
            zcopy[part, direction, tau, step - 1].wait_recv()
            value = value + zr[part, direction, tau, step - 1].astype(F32)
        zs[part, direction, tau, step] = value.astype(BF16)
        go(zcopy[part, direction, tau, step])

    def z_start(part, t):
        for h in range(4):
            value_in(3 if part == 1 else 2, h, t)
        for pair in range(4):
            z_part(part, t, pair, 1)
            if pair == 0:
                z_step(part, 0, 2 * t, 0)
                z_step(part, 1, 2 * t + 1, 0)
                z_step(part, 0, 2 * t + 1, 0)
            if pair == 1:
                z_step(part, 1, 2 * t, 0)

    def z_on(part, t, step):
        z_step(part, 0, 2 * t, step)
        z_step(part, 1, 2 * t + 1, step)
        z_step(part, 0, 2 * t + 1, step)
        z_step(part, 1, 2 * t, step)

    def z_end(part, t):
        for tau in (2 * t, 2 * t + 1):
            rows = slice(tau * 128, (tau + 1) * 128)
            value = zsum[part, POS[0], rows, :]
            for direction in (1 - tau % 2, tau % 2):
                step = (4 if direction == tau % 2 else 3) - 1
                zcopy[part, direction, tau, step].wait_recv()
                value = value + zr[part, direction, tau, step].astype(F32)
            zout[part, rows, :] = value.astype(BF16)

    out_copy = remote(zout.at[1], enc_out.at[s], ossem.at[0], orsem.at[0], n1)
    own_copy = pltpu.make_async_copy(zout.at[0], enc_out.at[s], ossem.at[1])

    gcopy = [remote(gs.at[i], gr.at[i], gssem.at[i], grsem.at[i], peer) for i in range(8)]

    def g_head(f, h):
        i = f * 4 + h
        va, vb = (0, 1) if f == 0 else (2, 3)
        for t in range(2):
            if f == 1:
                value_in(va, h, t)
            value_in(vb, h, t)
        gs[i] = (dot(et[0, 512:, :], val[va, h], 1, 0) + dot(et[1, 512:, :], val[vb, h], 1, 0)).astype(BF16)
        go(gcopy[i])
        gkeep[i] = dot(et[0, :512, :], val[va, h], 1, 0) + dot(et[1, :512, :], val[vb, h], 1, 0)

    xcopy = {}
    for i in range(8):
        for k in range(3):
            xcopy[i, k] = remote(xs.at[i, k], xr.at[i, k], xssem.at[i, k], xrsem.at[i, k], xdev[k])

    def x_send(f, h):
        i = f * 4 + h
        gcopy[i].wait_recv()
        for k in (1, 0, 2):
            rows = slice((k + 1) * 128, (k + 2) * 128)
            xs[i, k] = (gkeep[i, rows, :] + gr[i, rows, :].astype(F32)).astype(BF16)
            go(xcopy[i, k])

    fcopy, flocal = {}, {}
    for i in range(8):
        where = dev(x, c, m, z, m if i < 4 else 1 - m)
        fcopy[i] = remote(fs.at[i], val_out.at[s, i % 4], fssem.at[i], frsem.at[s, i % 4], where)
        flocal[i] = pltpu.make_async_copy(fs.at[i], val_out.at[s, i % 4], frsem.at[s, i % 4])

    def f_send(f, h):
        i = f * 4 + h
        value = gkeep[i, :128, :] + gr[i, :128, :].astype(F32)
        for k in range(3):
            xcopy[i, k].wait_recv()
            value = value + xr[i, k].astype(F32)
        fs[i] = value.astype(BF16)
        if f == 0:
            @pl.when(selfy)
            def _():
                flocal[i].start()

            @pl.when(jnp.logical_not(selfy))
            def _():
                fcopy[i].start()
        else:
            go(fcopy[i])

    def f_in(h):
        for half in range(2):
            remote(fs.at[h], val_out.at[half, h], fssem.at[h], frsem.at[half, h], n1).wait_recv()

    def value_on(to, i):
        if to == 3 and i < WINDOW:
            sent(w_in[i - 1])
        value_next(to, i)

    def weights_in():
        for copy in w_c.values():
            copy.wait_recv()

    steps = {
        "et": enc_first, "second": enc_second, "e": enc_in, "v": value_on, "won": weight_on, "wac": weight_across,
        "wdone": weights_in, "zf": z_first, "zs": z_start, "z": z_step, "ze": z_end, "out": lambda: go(out_copy),
        "g": g_head, "x": x_send, "f": f_send, "fin": f_in,
    }
    for what, *which in ORDER:
        steps[what](*which)
    own_copy.start()
    out_copy.wait_recv()
    for copy in sends:
        copy.wait_send()
    for i in range(4):
        @pl.when(jnp.logical_not(selfy))
        def _():
            fcopy[i].wait_send()
    own_copy.wait()


def finish(enc_in, val_in, eg_out, vg_out):
    for half in range(2):
        eg_out[:, half * 128 : (half + 1) * 128] = enc_in[half]
        for h in range(4):
            vg_out[0, half * 128 : (half + 1) * 128, h * 256 : (h + 1) * 256] = val_in[half, h].astype(F32)


def local(enc_states, value_weight, attn_weights, ctx_grad, prompt_lengths):
    anywhere = pl.BlockSpec(memory_space=pl.ANY)
    vmem = pl.BlockSpec(memory_space=pltpu.VMEM)
    dma = pltpu.SemaphoreType.DMA
    enc_halves, value_parts = pl.pallas_call(
        kernel,
        out_shape=(jax.ShapeDtypeStruct((2, 512, 128), BF16), jax.ShapeDtypeStruct((2, 4, 128, 256), BF16)),
        in_specs=[pl.BlockSpec(memory_space=pltpu.SMEM)] + [anywhere] * 4,
        out_specs=(anywhere, anywhere),
        scratch_shapes=[
            pltpu.VMEM((4, 256, 512), BF16),
            pltpu.VMEM((256, 1024), BF16),
            pltpu.VMEM((2, 8, 512, 128), BF16),
            pltpu.VMEM((2, 1024, 512), BF16),
            pltpu.VMEM((4, 4, 512, 256), BF16),
            pltpu.VMEM((2, 1024, 1024), BF16),
            pltpu.VMEM((2, 8, 512, 128), F32),
            pltpu.VMEM((2, 2, 4, 4, 128, 128), BF16),
            pltpu.VMEM((2, 2, 4, 4, 128, 128), BF16),
            pltpu.VMEM((8, 512, 256), F32),
            pltpu.VMEM((8, 512, 256), BF16),
            pltpu.VMEM((8, 512, 256), BF16),
            pltpu.VMEM((8, 3, 128, 256), BF16),
            pltpu.VMEM((8, 3, 128, 256), BF16),
            pltpu.VMEM((8, 128, 256), BF16),
            pltpu.VMEM((2, 512, 128), BF16),
            dma((6,)), dma((8,)),
            dma((2, 8, 2)), dma((2, 8, 2)),
            dma((4, 4, 2)), dma((4, 4, 2)),
            dma((8, 2)), dma((8, 2)),
            dma((2, 2, 4, 4)), dma((2, 2, 4, 4)),
            dma((8,)), dma((8,)),
            dma((8, 3)), dma((8, 3)),
            dma((8,)), dma((2, 4)),
            dma((2,)), dma((1,)),
        ],
        compiler_params=pltpu.CompilerParams(
            collective_id=0, has_side_effects=True, vmem_limit_bytes=60 * 2**20
        ),
        cost_estimate=pl.CostEstimate(flops=9 * 10**9, bytes_accessed=12 * 2**20, transcendentals=0),
    )(prompt_lengths, enc_states, value_weight, attn_weights, ctx_grad)
    return pl.pallas_call(
        finish,
        out_shape=(jax.ShapeDtypeStruct((512, 256), BF16), jax.ShapeDtypeStruct((1, 256, 1024), F32)),
        in_specs=[vmem, vmem],
        out_specs=(vmem, vmem),
    )(enc_halves, value_parts)


def solution(mesh):
    in_specs = (
        P("dp", ("section", "mp")),
        P("section", None, "mp"),
        P("section", "mp", "dp", None),
        P("section", "dp", "mp"),
        P("dp"),
    )
    out_specs = (P("dp", ("section", "mp")), P("section", "dp", "mp"))
    return jax.shard_map(local, mesh=mesh, in_specs=in_specs, out_specs=out_specs, check_vma=False)
```

```python
import jax
import jax.numpy as jnp
from jax import lax
from jax.experimental import pallas as pl
from jax.experimental.pallas import tpu as pltpu
from jax.sharding import PartitionSpec as P


MESH = pl.DeviceIdType.MESH
REL = (4, 3, 5, 2, 6, 1, 7, 0)
POS = {rel: slot for slot, rel in enumerate(REL)}
BF16 = jnp.bfloat16
F32 = jnp.float32
WINDOW = 8
ORDER = (
    ("second", 0), ("v", 3, 4), ("zf", 0, 1), ("v", 3, 1), ("v", 3, 2), ("v", 3, 3), ("zf", 0, 0), ("e", 0, 1, 0),
    ("second", 1), ("e", 0, 7, 0), ("won", 0), ("v", 3, 5), ("v", 3, 6), ("et", 1, 0), ("v", 3, 7), ("et", 0, 0),
    ("e", 0, 1, 1), ("e", 0, 7, 1), ("e", 1, 7, 0), ("e", 1, 1, 0), ("won", 1), ("e", 0, 2, 0), ("e", 1, 7, 1),
    ("e", 1, 1, 1), ("e", 0, 6, 0), ("v", 1, 8), ("wac", 1, 0), ("e", 0, 2, 1), ("e", 0, 6, 1), ("e", 1, 2, 0),
    ("e", 1, 6, 0), ("wac", 0, 0), ("wac", 2, 0), ("e", 0, 3, 0), ("e", 1, 6, 1), ("e", 1, 2, 1), ("e", 0, 5, 0),
    ("wac", 1, 1), ("v", 1, 9), ("zf", 1, 0), ("e", 0, 3, 1), ("e", 0, 5, 1), ("e", 1, 3, 0), ("e", 1, 5, 0),
    ("v", 3, 8), ("wac", 2, 1), ("v", 1, 10), ("wac", 0, 1), ("e", 0, 4, 0), ("e", 1, 5, 1), ("wdone",),
    ("e", 1, 3, 1), ("v", 3, 9), ("v", 1, 11), ("e", 0, 4, 1), ("zs", 1, 0), ("e", 1, 4, 0), ("v", 3, 10),
    ("e", 1, 4, 1), ("g", 0, 2), ("z", 1, 1, 0, 1), ("z", 1, 1, 1, 1), ("z", 1, 0, 0, 1), ("g", 0, 0), ("zf", 1, 1),
    ("x", 0, 2), ("z", 1, 0, 1, 1), ("v", 3, 11), ("g", 0, 3), ("x", 0, 0), ("g", 0, 1), ("z", 1, 1, 0, 2),
    ("zs", 1, 1), ("x", 0, 3), ("z", 1, 1, 1, 2), ("z", 1, 0, 0, 2), ("x", 0, 1), ("z", 1, 0, 1, 2), ("g", 1, 0),
    ("z", 1, 0, 2, 1), ("z", 1, 1, 2, 1), ("x", 1, 0), ("z", 1, 1, 3, 1), ("z", 1, 0, 3, 1), ("g", 1, 1),
    ("z", 1, 0, 0, 3), ("z", 1, 1, 1, 3), ("x", 1, 1), ("z", 1, 0, 2, 2), ("z", 1, 1, 2, 2), ("zs", 0, 0),
    ("z", 1, 1, 3, 2), ("z", 1, 0, 3, 2), ("g", 1, 2), ("ze", 1, 0), ("f", 0, 0), ("zs", 0, 1), ("f", 0, 2),
    ("x", 1, 2), ("z", 0, 1, 0, 1), ("z", 0, 0, 0, 1), ("z", 1, 0, 2, 3), ("g", 1, 3), ("z", 0, 1, 1, 1),
    ("z", 0, 0, 1, 1), ("f", 0, 3), ("z", 1, 1, 3, 3), ("f", 0, 1), ("x", 1, 3), ("f", 1, 0), ("z", 0, 1, 2, 1),
    ("z", 0, 0, 2, 1), ("z", 0, 0, 3, 1), ("z", 0, 1, 3, 1), ("z", 0, 1, 0, 2), ("z", 0, 0, 0, 2), ("z", 0, 1, 1, 2),
    ("f", 1, 1), ("z", 0, 0, 1, 2), ("ze", 1, 1), ("out",), ("fin", 0), ("z", 0, 1, 2, 2), ("z", 0, 0, 2, 2),
    ("z", 0, 1, 3, 2), ("z", 0, 0, 3, 2), ("z", 0, 0, 0, 3), ("f", 1, 2), ("z", 0, 1, 1, 3), ("fin", 1),
    ("z", 0, 0, 2, 3), ("z", 0, 1, 3, 3), ("f", 1, 3), ("ze", 0, 0), ("fin", 2), ("ze", 0, 1), ("fin", 3),
)


def dot(a, b, ca, cb):
    return lax.dot_general(a, b, (((ca,), (cb,)), ((), ())), preferred_element_type=F32)


def kernel(
    lens, enc, weight, attn, ctx, enc_out, val_out,
    attn_v, ctx_v, ebuf, et, val, wq, zsum, zs, zr, gkeep, gs, gr, xs, xr, fs, zout,
    lsem, wlsem, essem, ersem, vssem, vrsem, wssem, wrsem, zssem, zrsem,
    gssem, grsem, xssem, xrsem, fssem, frsem, ossem, orsem,
):
    dp, z, m = lax.axis_index("dp"), lax.axis_index("section"), lax.axis_index("mp")
    x, s, c = dp // 4, (dp // 2) % 2, dp % 2

    def dev(x_, s_, c_, z_, m_):
        return (x_ * 4 + s_ * 2 + c_, z_, m_)

    n1 = dev(x, 1 - s, c, z, m)
    n2 = dev(x, 1 - s, c, z, 1 - m)
    peer = dev(x, s, 1 - c, z, m)
    zdev = (dev(x, s, c, (z + 1) % 8, m), dev(x, s, c, (z + 7) % 8, m))
    xdev = tuple(dev((x + k) % 4, s, c, z, m) for k in (1, 2, 3))
    selfy = jnp.logical_and(s == c, c == m)
    same = selfy.astype(jnp.int32)
    sends = []

    def remote(src, dst, ss, rs, where):
        return pltpu.make_async_remote_copy(
            src_ref=src, dst_ref=dst, send_sem=ss, recv_sem=rs, device_id=where, device_id_type=MESH
        )

    def go(copy):
        copy.start()
        sends.append(copy)

    def sent(copy):
        copy.wait_send()
        sends[:] = [other for other in sends if other is not copy]

    own_enc = pltpu.make_async_copy(
        enc.at[:, pl.ds(pl.multiple_of(s * 128, 128), 128)], ebuf.at[0, 0], lsem.at[0]
    )
    own_ctx = pltpu.make_async_copy(ctx.at[0], ctx_v, lsem.at[1])
    own_attn = [pltpu.make_async_copy(attn.at[0, h], attn_v.at[h], lsem.at[2 + h]) for h in range(4)]
    own_enc.start()
    own_attn[0].start()
    own_ctx.start()
    for h in range(1, 4):
        own_attn[h].start()

    def weight_rows(slot_rel, m_, s_):
        layer = (z + slot_rel) % 8
        return pl.ds(pl.multiple_of((2 * layer + m_) * 256 + s_ * 128, 128), 128)

    own_w = []
    for slot in range(8):
        own_w.append(
            pltpu.make_async_copy(
                weight.at[0, weight_rows(REL[slot], m, s), :], wq.at[0, pl.ds(slot * 128, 128), :], wlsem.at[slot]
            )
        )

    barrier = pltpu.get_barrier_semaphore()
    for where in (n1, n2, peer) + zdev + xdev:
        pl.semaphore_signal(barrier, inc=1, device_id=where, device_id_type=MESH)
    for half in range(2):
        @pl.when(jnp.logical_not(jnp.logical_and(selfy, s == half)))
        def _():
            pl.semaphore_signal(barrier, inc=1, device_id=dev(x, half, s, z, c), device_id_type=MESH)
    pl.semaphore_wait(barrier, 10 - same)

    row_half = (pl.ds(0, 256), pl.ds(256, 256))
    pre = []
    for u in range(2):
        src = enc.at[row_half[u], pl.ds(pl.multiple_of((1 - s) * 128, 128), 128)]
        pre.append(remote(src, ebuf.at[1, 0, row_half[u], :], essem.at[1, 0, u], ersem.at[1, 0, u], n1))
        go(pre[u])
    own_enc.wait()

    ecopy = {}
    for part in range(2):
        for u in range(2):
            for direction in range(2):
                for step in range(4 if (part == u) == (direction == 0) else 3):
                    src = (8 - step) % 8 if direction else step
                    to = 7 - step if direction else step + 1
                    ecopy[part, to, u] = remote(
                        ebuf.at[part, src, row_half[u], :], ebuf.at[part, to, row_half[u], :],
                        essem.at[part, to, u], ersem.at[part, to, u], zdev[direction],
                    )
    for u in range(2):
        go(ecopy[0, 1, u])
        go(ecopy[0, 7, u])

    piece = 2 * x + c
    piece_rel = 0
    for slot in range(8):
        piece_rel = jnp.where(piece == slot, REL[slot], piece_rel)
    layer_rows = (2 * ((z + piece_rel) % 8) + 1 - m) * 256 + (1 - s) * 128

    def weight_piece(owner, j):
        return wq.at[1, pl.ds(pl.multiple_of(owner * 128 + j * 64, 64), 64), :]

    w_in = []
    for j in range(2):
        rows = pl.ds(pl.multiple_of(layer_rows + j * 64, 64), 64)
        w_in.append(remote(weight.at[0, rows, :], weight_piece(piece, j), wssem.at[0, j], wrsem.at[0, j], n2))
        go(w_in[j])
    for copy in own_w:
        copy.start()


    def value_copy(src, to, h, t, where):
        return remote(
            val.at[src, h, row_half[t], :], val.at[to, h, row_half[t], :],
            vssem.at[to, h, t], vrsem.at[to, h, t], where,
        )

    vcopy = {}
    for h in range(4):
        for t in range(2):
            vcopy[1, h, t] = value_copy(0, 1, h, t, n1)
            vcopy[3, h, t] = value_copy(0, 3, h, t, n2)
            vcopy[2, h, t] = value_copy(3, 2, h, t, n1) if t == 0 else value_copy(1, 2, h, t, n2)
    queues = {}
    for to, through in ((1, 0), (3, 1)):
        queues[to] = [(to, h, t) for t in range(2) for h in range(4)] + [(2, h, through) for h in range(4)]
    arrived = set()

    def value_in(*key):
        if key not in arrived:
            arrived.add(key)
            vcopy[key].wait_recv()

    def value_next(to, i):
        if i >= WINDOW:
            sent(vcopy[queues[to][i - WINDOW]])
        key = queues[to][i]
        if key[0] == 2:
            value_in(4 - to, key[1], key[2])
        go(vcopy[key])

    own_ctx.wait()
    keep = (lax.broadcasted_iota(jnp.int32, (512, 256), 0) < lens[0]).astype(F32)
    for h in range(4):
        own_attn[h].wait()
        raw = dot(attn_v[h], ctx_v[:, h * 256 : (h + 1) * 256], 0, 0)
        val[0, h] = (raw * keep).astype(BF16)
        if h < WINDOW:
            value_next(1, h)
        if h == 0:
            value_next(3, 0)
    for i in range(4, WINDOW):
        value_next(1, i)

    def put_et(part, rel, u):
        layer = (z + 8 - rel) % 8
        row = ((layer + c) % 2 * 4 + (layer // 2 + 4 - x) % 4) * 128
        columns = slice(u * 256, (u + 1) * 256)
        et[part, pl.ds(pl.multiple_of(row, 128), 128), columns] = ebuf[part, rel, columns, :].T

    def enc_first(part, rel):
        for u in range(2):
            put_et(part, rel, u)

    def enc_second(u):
        pre[u].wait_recv()
        go(ecopy[1, 1, u])
        go(ecopy[1, 7, u])

    def enc_in(part, rel, u):
        ecopy[part, rel, u].wait_recv()
        top = 4 if part == u else 3
        if rel < top:
            go(ecopy[part, rel + 1, u])
        elif rel > top + 1:
            go(ecopy[part, rel - 1, u])
        put_et(part, rel, u)

    def z_part(part, t, pair, which):
        slot = {(0, 0): 0, (0, 1): 2, (1, 0): 1, (1, 1): 3}[part, which]
        rows = wq.at[which, pl.ds(pair * 256, 256), :]
        acc = None
        for h in range(4):
            term = dot(val[slot, h, t * 256 : (t + 1) * 256, :], rows[:, h * 256 : (h + 1) * 256], 1, 1)
            acc = term if acc is None else acc + term
        for i in range(2):
            half = acc[:, i * 128 : (i + 1) * 128]
            if which == 0:
                zsum[part, 2 * pair + i, t * 256 : (t + 1) * 256, :] = half
            else:
                zsum[part, 2 * pair + i, t * 256 : (t + 1) * 256, :] += half

    own_w_waits = list(own_w)

    def z_first(part, t):
        while own_w_waits:
            own_w_waits.pop().wait()
        for h in range(4):
            if part == 1:
                value_in(1, h, t)
        for pair in range(4):
            z_part(part, t, pair, 0)

    w_x, w_c = {}, {}
    for j in range(2):
        for k in range(3):
            ref = weight_piece(piece, j)
            w_x[k, j] = remote(ref, ref, wssem.at[1 + k, j], wrsem.at[1 + k, j], xdev[k])
        for k in range(4):
            ref = weight_piece(2 * ((x + 4 - k) % 4) + c, j)
            w_c[k, j] = remote(ref, ref, wssem.at[4 + k, j], wrsem.at[4 + k, j], peer)

    def weight_on(j):
        w_in[j].wait_recv()
        for k in (1, 0, 2):
            go(w_x[k, j])
        go(w_c[0, j])

    def weight_across(k, j):
        w_x[k, j].wait_recv()
        go(w_c[k + 1, j])

    zcopy = {}
    for part in range(2):
        for direction in range(2):
            for tau in range(4):
                for step in range(4 if direction == tau % 2 else 3):
                    zcopy[part, direction, tau, step] = remote(
                        zs.at[part, direction, tau, step], zr.at[part, direction, tau, step],
                        zssem.at[part, direction, tau, step], zrsem.at[part, direction, tau, step], zdev[direction],
                    )

    def z_step(part, direction, tau, step):
        length = 4 if direction == tau % 2 else 3
        if step >= length:
            return
        ahead = length - step
        slot = POS[(8 - ahead) % 8 if direction else ahead]
        value = zsum[part, slot, tau * 128 : (tau + 1) * 128, :]
        if step > 0:
            zcopy[part, direction, tau, step - 1].wait_recv()
            value = value + zr[part, direction, tau, step - 1].astype(F32)
        zs[part, direction, tau, step] = value.astype(BF16)
        go(zcopy[part, direction, tau, step])

    def z_start(part, t):
        for h in range(4):
            value_in(3 if part == 1 else 2, h, t)
        for pair in range(4):
            z_part(part, t, pair, 1)
            if pair == 0:
                z_step(part, 0, 2 * t, 0)
                z_step(part, 1, 2 * t + 1, 0)
                z_step(part, 0, 2 * t + 1, 0)
            if pair == 1:
                z_step(part, 1, 2 * t, 0)

    def z_on(part, t, step):
        z_step(part, 0, 2 * t, step)
        z_step(part, 1, 2 * t + 1, step)
        z_step(part, 0, 2 * t + 1, step)
        z_step(part, 1, 2 * t, step)

    def z_end(part, t):
        for tau in (2 * t, 2 * t + 1):
            rows = slice(tau * 128, (tau + 1) * 128)
            value = zsum[part, POS[0], rows, :]
            for direction in (1 - tau % 2, tau % 2):
                step = (4 if direction == tau % 2 else 3) - 1
                zcopy[part, direction, tau, step].wait_recv()
                value = value + zr[part, direction, tau, step].astype(F32)
            zout[part, rows, :] = value.astype(BF16)

    out_copy = remote(zout.at[1], enc_out.at[s], ossem.at[0], orsem.at[0], n1)
    own_copy = pltpu.make_async_copy(zout.at[0], enc_out.at[s], ossem.at[1])

    gcopy = [remote(gs.at[i], gr.at[i], gssem.at[i], grsem.at[i], peer) for i in range(8)]

    def g_head(f, h):
        i = f * 4 + h
        va, vb = (0, 1) if f == 0 else (2, 3)
        for t in range(2):
            if f == 1:
                value_in(va, h, t)
            value_in(vb, h, t)
        gs[i] = (dot(et[0, 512:, :], val[va, h], 1, 0) + dot(et[1, 512:, :], val[vb, h], 1, 0)).astype(BF16)
        go(gcopy[i])
        gkeep[i] = dot(et[0, :512, :], val[va, h], 1, 0) + dot(et[1, :512, :], val[vb, h], 1, 0)

    xcopy = {}
    for i in range(8):
        for k in range(3):
            xcopy[i, k] = remote(xs.at[i, k], xr.at[i, k], xssem.at[i, k], xrsem.at[i, k], xdev[k])

    def x_send(f, h):
        i = f * 4 + h
        gcopy[i].wait_recv()
        for k in (1, 0, 2):
            rows = slice((k + 1) * 128, (k + 2) * 128)
            xs[i, k] = (gkeep[i, rows, :] + gr[i, rows, :].astype(F32)).astype(BF16)
            go(xcopy[i, k])

    fcopy, flocal = {}, {}
    for i in range(8):
        where = dev(x, c, m, z, m if i < 4 else 1 - m)
        fcopy[i] = remote(fs.at[i], val_out.at[s, i % 4], fssem.at[i], frsem.at[s, i % 4], where)
        flocal[i] = pltpu.make_async_copy(fs.at[i], val_out.at[s, i % 4], frsem.at[s, i % 4])

    def f_send(f, h):
        i = f * 4 + h
        value = gkeep[i, :128, :] + gr[i, :128, :].astype(F32)
        for k in range(3):
            xcopy[i, k].wait_recv()
            value = value + xr[i, k].astype(F32)
        fs[i] = value.astype(BF16)
        if f == 0:
            @pl.when(selfy)
            def _():
                flocal[i].start()

            @pl.when(jnp.logical_not(selfy))
            def _():
                fcopy[i].start()
        else:
            go(fcopy[i])

    def f_in(h):
        for half in range(2):
            remote(fs.at[h], val_out.at[half, h], fssem.at[h], frsem.at[half, h], n1).wait_recv()

    w_left = [0, 1]

    def value_on(to, i):
        if to == 3 and i < WINDOW:
            j = 0 if i <= WINDOW // 2 else 1
            if j in w_left:
                w_left.remove(j)
                sent(w_in[j])
        value_next(to, i)

    def weights_in():
        for copy in w_c.values():
            copy.wait_recv()

    steps = {
        "et": enc_first, "second": enc_second, "e": enc_in, "v": value_on, "won": weight_on, "wac": weight_across,
        "wdone": weights_in, "zf": z_first, "zs": z_start, "z": z_step, "ze": z_end, "out": lambda: go(out_copy),
        "g": g_head, "x": x_send, "f": f_send, "fin": f_in,
    }
    for what, *which in ORDER:
        steps[what](*which)
    own_copy.start()
    out_copy.wait_recv()
    for copy in sends:
        copy.wait_send()
    for i in range(4):
        @pl.when(jnp.logical_not(selfy))
        def _():
            fcopy[i].wait_send()
    own_copy.wait()


def finish(enc_in, val_in, eg_out, vg_out):
    for half in range(2):
        eg_out[:, half * 128 : (half + 1) * 128] = enc_in[half]
        for h in range(4):
            vg_out[0, half * 128 : (half + 1) * 128, h * 256 : (h + 1) * 256] = val_in[half, h].astype(F32)


def local(enc_states, value_weight, attn_weights, ctx_grad, prompt_lengths):
    anywhere = pl.BlockSpec(memory_space=pl.ANY)
    vmem = pl.BlockSpec(memory_space=pltpu.VMEM)
    dma = pltpu.SemaphoreType.DMA
    enc_halves, value_parts = pl.pallas_call(
        kernel,
        out_shape=(jax.ShapeDtypeStruct((2, 512, 128), BF16), jax.ShapeDtypeStruct((2, 4, 128, 256), BF16)),
        in_specs=[pl.BlockSpec(memory_space=pltpu.SMEM)] + [anywhere] * 4,
        out_specs=(anywhere, anywhere),
        scratch_shapes=[
            pltpu.VMEM((4, 256, 512), BF16),
            pltpu.VMEM((256, 1024), BF16),
            pltpu.VMEM((2, 8, 512, 128), BF16),
            pltpu.VMEM((2, 1024, 512), BF16),
            pltpu.VMEM((4, 4, 512, 256), BF16),
            pltpu.VMEM((2, 1024, 1024), BF16),
            pltpu.VMEM((2, 8, 512, 128), F32),
            pltpu.VMEM((2, 2, 4, 4, 128, 128), BF16),
            pltpu.VMEM((2, 2, 4, 4, 128, 128), BF16),
            pltpu.VMEM((8, 512, 256), F32),
            pltpu.VMEM((8, 512, 256), BF16),
            pltpu.VMEM((8, 512, 256), BF16),
            pltpu.VMEM((8, 3, 128, 256), BF16),
            pltpu.VMEM((8, 3, 128, 256), BF16),
            pltpu.VMEM((8, 128, 256), BF16),
            pltpu.VMEM((2, 512, 128), BF16),
            dma((6,)), dma((8,)),
            dma((2, 8, 2)), dma((2, 8, 2)),
            dma((4, 4, 2)), dma((4, 4, 2)),
            dma((8, 2)), dma((8, 2)),
            dma((2, 2, 4, 4)), dma((2, 2, 4, 4)),
            dma((8,)), dma((8,)),
            dma((8, 3)), dma((8, 3)),
            dma((8,)), dma((2, 4)),
            dma((2,)), dma((1,)),
        ],
        compiler_params=pltpu.CompilerParams(
            collective_id=0, has_side_effects=True, vmem_limit_bytes=60 * 2**20
        ),
        cost_estimate=pl.CostEstimate(flops=9 * 10**9, bytes_accessed=12 * 2**20, transcendentals=0),
    )(prompt_lengths, enc_states, value_weight, attn_weights, ctx_grad)
    return pl.pallas_call(
        finish,
        out_shape=(jax.ShapeDtypeStruct((512, 256), BF16), jax.ShapeDtypeStruct((1, 256, 1024), F32)),
        in_specs=[vmem, vmem],
        out_specs=(vmem, vmem),
    )(enc_halves, value_parts)


def solution(mesh):
    in_specs = (
        P("dp", ("section", "mp")),
        P("section", None, "mp"),
        P("section", "mp", "dp", None),
        P("section", "dp", "mp"),
        P("dp"),
    )
    out_specs = (P("dp", ("section", "mp")), P("section", "dp", "mp"))
    return jax.shard_map(local, mesh=mesh, in_specs=in_specs, out_specs=out_specs, check_vma=False)
```

```python
import jax
import jax.numpy as jnp
from jax import lax
from jax.experimental import pallas as pl
from jax.experimental.pallas import tpu as pltpu
from jax.sharding import PartitionSpec as P


MESH = pl.DeviceIdType.MESH
REL = (4, 3, 5, 2, 6, 1, 7, 0)
POS = {rel: slot for slot, rel in enumerate(REL)}
BF16 = jnp.bfloat16
F32 = jnp.float32
WINDOW = 5
ORDER = (
    ("v", 3, 1), ("second", 0), ("v", 3, 2), ("zf", 0, 1), ("et", 0, 0), ("zf", 0, 0), ("e", 0, 1, 0), ("second", 1),
    ("won", 0), ("v", 1, 5), ("v", 3, 3), ("v", 3, 4), ("e", 0, 7, 0), ("et", 1, 0), ("e", 0, 1, 1), ("e", 0, 7, 1),
    ("e", 1, 1, 0), ("e", 1, 7, 0), ("won", 1), ("v", 3, 5), ("v", 1, 6), ("e", 0, 2, 0), ("e", 1, 7, 1),
    ("e", 1, 1, 1), ("e", 0, 6, 0), ("v", 3, 6), ("v", 1, 7), ("wac", 1, 0), ("e", 0, 2, 1), ("e", 0, 6, 1),
    ("e", 1, 2, 0), ("e", 1, 6, 0), ("wac", 2, 0), ("wac", 0, 0), ("v", 1, 8), ("v", 3, 7), ("e", 0, 3, 0),
    ("e", 1, 6, 1), ("e", 1, 2, 1), ("e", 0, 5, 0), ("v", 3, 8), ("wac", 1, 1), ("e", 0, 3, 1), ("e", 0, 5, 1),
    ("e", 1, 3, 0), ("e", 1, 5, 0), ("wac", 2, 1), ("wac", 0, 1), ("v", 1, 10), ("zf", 1, 0), ("e", 0, 4, 0),
    ("e", 1, 5, 1), ("wdone",), ("e", 1, 3, 1), ("v", 3, 10), ("zs", 1, 0), ("e", 0, 4, 1), ("e", 1, 4, 0),
    ("v", 1, 9), ("e", 1, 4, 1), ("g", 0, 1), ("z", 1, 1, 0, 1), ("g", 0, 0), ("v", 3, 9), ("z", 1, 0, 1, 1),
    ("z", 1, 1, 1, 1), ("g", 0, 2), ("z", 1, 0, 0, 1), ("x", 0, 1), ("v", 1, 11), ("x", 0, 0), ("x", 0, 2),
    ("z", 1, 1, 0, 2), ("v", 3, 11), ("zf", 1, 1), ("g", 0, 3), ("z", 1, 1, 1, 2), ("z", 1, 0, 1, 2),
    ("z", 1, 0, 0, 2), ("x", 0, 3), ("zs", 1, 1), ("z", 1, 1, 1, 3), ("z", 1, 0, 0, 3), ("z", 1, 0, 2, 1),
    ("z", 1, 1, 2, 1), ("z", 1, 0, 3, 1), ("z", 1, 1, 3, 1), ("g", 1, 0), ("zs", 0, 0), ("ze", 1, 0), ("x", 1, 0),
    ("z", 1, 1, 2, 2), ("z", 1, 0, 2, 2), ("z", 1, 0, 3, 2), ("z", 1, 1, 3, 2), ("g", 1, 1), ("g", 1, 2),
    ("z", 0, 1, 0, 1), ("z", 0, 0, 0, 1), ("x", 1, 1), ("z", 0, 1, 1, 1), ("z", 0, 0, 1, 1), ("zs", 0, 1),
    ("z", 1, 0, 2, 3), ("x", 1, 2), ("f", 0, 0), ("z", 1, 1, 3, 3), ("g", 1, 3), ("f", 0, 1), ("f", 1, 0),
    ("f", 0, 3), ("z", 0, 1, 0, 2), ("z", 0, 0, 0, 2), ("f", 0, 2), ("z", 0, 1, 1, 2), ("z", 0, 0, 1, 2), ("x", 1, 3),
    ("z", 0, 1, 2, 1), ("z", 0, 0, 2, 1), ("z", 0, 1, 3, 1), ("z", 0, 0, 3, 1), ("f", 1, 1), ("ze", 1, 1), ("out",),
    ("z", 0, 0, 0, 3), ("fin", 0), ("z", 0, 1, 1, 3), ("z", 0, 1, 2, 2), ("z", 0, 0, 2, 2), ("f", 1, 2),
    ("z", 0, 1, 3, 2), ("z", 0, 0, 3, 2), ("fin", 1), ("ze", 0, 0), ("f", 1, 3), ("z", 0, 0, 2, 3), ("z", 0, 1, 3, 3),
    ("fin", 2), ("fin", 3), ("ze", 0, 1),
)


def dot(a, b, ca, cb):
    return lax.dot_general(a, b, (((ca,), (cb,)), ((), ())), preferred_element_type=F32)


def kernel(
    lens, enc, weight, attn, ctx, enc_out, val_out,
    attn_v, ctx_v, ebuf, et, val, wq, zsum, zs, zr, gkeep, gs, gr, xs, xr, fs, zout,
    lsem, wlsem, essem, ersem, vssem, vrsem, wssem, wrsem, zssem, zrsem,
    gssem, grsem, xssem, xrsem, fssem, frsem, ossem, orsem,
):
    dp, z, m = lax.axis_index("dp"), lax.axis_index("section"), lax.axis_index("mp")
    x, s, c = dp // 4, (dp // 2) % 2, dp % 2

    def dev(x_, s_, c_, z_, m_):
        return (x_ * 4 + s_ * 2 + c_, z_, m_)

    n1 = dev(x, 1 - s, c, z, m)
    n2 = dev(x, 1 - s, c, z, 1 - m)
    peer = dev(x, s, 1 - c, z, m)
    zdev = (dev(x, s, c, (z + 1) % 8, m), dev(x, s, c, (z + 7) % 8, m))
    xdev = tuple(dev((x + k) % 4, s, c, z, m) for k in (1, 2, 3))
    selfy = jnp.logical_and(s == c, c == m)
    same = selfy.astype(jnp.int32)
    sends = []

    def remote(src, dst, ss, rs, where):
        return pltpu.make_async_remote_copy(
            src_ref=src, dst_ref=dst, send_sem=ss, recv_sem=rs, device_id=where, device_id_type=MESH
        )

    def go(copy):
        copy.start()
        sends.append(copy)

    def sent(copy):
        copy.wait_send()
        sends[:] = [other for other in sends if other is not copy]

    own_enc = pltpu.make_async_copy(
        enc.at[:, pl.ds(pl.multiple_of(s * 128, 128), 128)], ebuf.at[0, 0], lsem.at[0]
    )
    own_ctx = pltpu.make_async_copy(ctx.at[0], ctx_v, lsem.at[1])
    own_attn = [pltpu.make_async_copy(attn.at[0, h], attn_v.at[h], lsem.at[2 + h]) for h in range(4)]
    own_enc.start()
    own_attn[0].start()
    own_ctx.start()
    for h in range(1, 4):
        own_attn[h].start()

    def weight_rows(slot_rel, m_, s_):
        layer = (z + slot_rel) % 8
        return pl.ds(pl.multiple_of((2 * layer + m_) * 256 + s_ * 128, 128), 128)

    own_w = []
    for slot in range(8):
        own_w.append(
            pltpu.make_async_copy(
                weight.at[0, weight_rows(REL[slot], m, s), :], wq.at[0, pl.ds(slot * 128, 128), :], wlsem.at[slot]
            )
        )

    barrier = pltpu.get_barrier_semaphore()
    for where in (n1, n2, peer) + zdev + xdev:
        pl.semaphore_signal(barrier, inc=1, device_id=where, device_id_type=MESH)
    for half in range(2):
        @pl.when(jnp.logical_not(jnp.logical_and(selfy, s == half)))
        def _():
            pl.semaphore_signal(barrier, inc=1, device_id=dev(x, half, s, z, c), device_id_type=MESH)
    pl.semaphore_wait(barrier, 10 - same)

    row_half = (pl.ds(0, 256), pl.ds(256, 256))
    pre = []
    for u in range(2):
        src = enc.at[row_half[u], pl.ds(pl.multiple_of((1 - s) * 128, 128), 128)]
        pre.append(remote(src, ebuf.at[1, 0, row_half[u], :], essem.at[1, 0, u], ersem.at[1, 0, u], n1))
        go(pre[u])
    own_enc.wait()

    ecopy = {}
    for part in range(2):
        for u in range(2):
            for direction in range(2):
                for step in range(4 if (part == u) == (direction == 0) else 3):
                    src = (8 - step) % 8 if direction else step
                    to = 7 - step if direction else step + 1
                    ecopy[part, to, u] = remote(
                        ebuf.at[part, src, row_half[u], :], ebuf.at[part, to, row_half[u], :],
                        essem.at[part, to, u], ersem.at[part, to, u], zdev[direction],
                    )
    for u in range(2):
        go(ecopy[0, 1, u])
        go(ecopy[0, 7, u])

    piece = 2 * x + c
    piece_rel = 0
    for slot in range(8):
        piece_rel = jnp.where(piece == slot, REL[slot], piece_rel)
    layer_rows = (2 * ((z + piece_rel) % 8) + 1 - m) * 256 + (1 - s) * 128

    def weight_piece(owner, j):
        return wq.at[1, pl.ds(pl.multiple_of(owner * 128 + j * 64, 64), 64), :]

    w_in = []
    for j in range(2):
        rows = pl.ds(pl.multiple_of(layer_rows + j * 64, 64), 64)
        w_in.append(remote(weight.at[0, rows, :], weight_piece(piece, j), wssem.at[0, j], wrsem.at[0, j], n2))
        go(w_in[j])
    for copy in own_w:
        copy.start()


    def value_copy(src, to, h, t, where):
        return remote(
            val.at[src, h, row_half[t], :], val.at[to, h, row_half[t], :],
            vssem.at[to, h, t], vrsem.at[to, h, t], where,
        )

    vcopy = {}
    for h in range(4):
        for t in range(2):
            vcopy[1, h, t] = value_copy(0, 1, h, t, n1)
            vcopy[3, h, t] = value_copy(0, 3, h, t, n2)
            vcopy[2, h, t] = value_copy(3, 2, h, t, n1) if h < 2 else value_copy(1, 2, h, t, n2)
    queues = {}
    for to, through in ((1, (0, 1)), (3, (2, 3))):
        queues[to] = [(to, h, t) for t in range(2) for h in range(4)] + [(2, h, t) for h in through for t in range(2)]
    arrived = set()

    def value_in(*key):
        if key not in arrived:
            arrived.add(key)
            vcopy[key].wait_recv()

    def value_next(to, i):
        if i >= WINDOW:
            sent(vcopy[queues[to][i - WINDOW]])
        key = queues[to][i]
        if key[0] == 2:
            value_in(4 - to, key[1], key[2])
        go(vcopy[key])

    own_ctx.wait()
    keep = (lax.broadcasted_iota(jnp.int32, (512, 256), 0) < lens[0]).astype(F32)
    for h in range(4):
        own_attn[h].wait()
        raw = dot(attn_v[h], ctx_v[:, h * 256 : (h + 1) * 256], 0, 0)
        val[0, h] = (raw * keep).astype(BF16)
        if h < WINDOW:
            value_next(1, h)
        if h == 0:
            value_next(3, 0)
    for i in range(4, WINDOW):
        value_next(1, i)

    def put_et(part, rel, u):
        layer = (z + 8 - rel) % 8
        row = ((layer + c) % 2 * 4 + (layer // 2 + 4 - x) % 4) * 128
        columns = slice(u * 256, (u + 1) * 256)
        et[part, pl.ds(pl.multiple_of(row, 128), 128), columns] = ebuf[part, rel, columns, :].T

    def enc_first(part, rel):
        for u in range(2):
            put_et(part, rel, u)

    def enc_second(u):
        pre[u].wait_recv()
        go(ecopy[1, 1, u])
        go(ecopy[1, 7, u])

    def enc_in(part, rel, u):
        ecopy[part, rel, u].wait_recv()
        top = 4 if part == u else 3
        if rel < top:
            go(ecopy[part, rel + 1, u])
        elif rel > top + 1:
            go(ecopy[part, rel - 1, u])
        put_et(part, rel, u)

    def z_part(part, t, pair, which):
        slot = {(0, 0): 0, (0, 1): 2, (1, 0): 1, (1, 1): 3}[part, which]
        rows = wq.at[which, pl.ds(pair * 256, 256), :]
        acc = None
        for h in range(4):
            term = dot(val[slot, h, t * 256 : (t + 1) * 256, :], rows[:, h * 256 : (h + 1) * 256], 1, 1)
            acc = term if acc is None else acc + term
        for i in range(2):
            half = acc[:, i * 128 : (i + 1) * 128]
            if which == 0:
                zsum[part, 2 * pair + i, t * 256 : (t + 1) * 256, :] = half
            else:
                zsum[part, 2 * pair + i, t * 256 : (t + 1) * 256, :] += half

    own_w_waits = list(own_w)

    def z_first(part, t):
        while own_w_waits:
            own_w_waits.pop().wait()
        for h in range(4):
            if part == 1:
                value_in(1, h, t)
        for pair in range(4):
            z_part(part, t, pair, 0)

    w_x, w_c = {}, {}
    for j in range(2):
        for k in range(3):
            ref = weight_piece(piece, j)
            w_x[k, j] = remote(ref, ref, wssem.at[1 + k, j], wrsem.at[1 + k, j], xdev[k])
        for k in range(4):
            ref = weight_piece(2 * ((x + 4 - k) % 4) + c, j)
            w_c[k, j] = remote(ref, ref, wssem.at[4 + k, j], wrsem.at[4 + k, j], peer)

    def weight_on(j):
        w_in[j].wait_recv()
        for k in (1, 0, 2):
            go(w_x[k, j])
        go(w_c[0, j])

    def weight_across(k, j):
        w_x[k, j].wait_recv()
        go(w_c[k + 1, j])

    zcopy = {}
    for part in range(2):
        for direction in range(2):
            for tau in range(4):
                for step in range(4 if direction == tau % 2 else 3):
                    zcopy[part, direction, tau, step] = remote(
                        zs.at[part, direction, tau, step], zr.at[part, direction, tau, step],
                        zssem.at[part, direction, tau, step], zrsem.at[part, direction, tau, step], zdev[direction],
                    )

    def z_step(part, direction, tau, step):
        length = 4 if direction == tau % 2 else 3
        if step >= length:
            return
        ahead = length - step
        slot = POS[(8 - ahead) % 8 if direction else ahead]
        value = zsum[part, slot, tau * 128 : (tau + 1) * 128, :]
        if step > 0:
            zcopy[part, direction, tau, step - 1].wait_recv()
            value = value + zr[part, direction, tau, step - 1].astype(F32)
        zs[part, direction, tau, step] = value.astype(BF16)
        go(zcopy[part, direction, tau, step])

    def z_start(part, t):
        for h in range(4):
            value_in(3 if part == 1 else 2, h, t)
        for pair in range(4):
            z_part(part, t, pair, 1)
            if pair == 0:
                z_step(part, 0, 2 * t, 0)
                z_step(part, 1, 2 * t + 1, 0)
                z_step(part, 0, 2 * t + 1, 0)
            if pair == 1:
                z_step(part, 1, 2 * t, 0)

    def z_on(part, t, step):
        z_step(part, 0, 2 * t, step)
        z_step(part, 1, 2 * t + 1, step)
        z_step(part, 0, 2 * t + 1, step)
        z_step(part, 1, 2 * t, step)

    def z_end(part, t):
        for tau in (2 * t, 2 * t + 1):
            rows = slice(tau * 128, (tau + 1) * 128)
            value = zsum[part, POS[0], rows, :]
            for direction in (1 - tau % 2, tau % 2):
                step = (4 if direction == tau % 2 else 3) - 1
                zcopy[part, direction, tau, step].wait_recv()
                value = value + zr[part, direction, tau, step].astype(F32)
            zout[part, rows, :] = value.astype(BF16)

    out_copy = remote(zout.at[1], enc_out.at[s], ossem.at[0], orsem.at[0], n1)
    own_copy = pltpu.make_async_copy(zout.at[0], enc_out.at[s], ossem.at[1])

    gcopy = [remote(gs.at[i], gr.at[i], gssem.at[i], grsem.at[i], peer) for i in range(8)]

    def g_head(f, h):
        i = f * 4 + h
        va, vb = (0, 1) if f == 0 else (2, 3)
        for t in range(2):
            if f == 1:
                value_in(va, h, t)
            value_in(vb, h, t)
        gs[i] = (dot(et[0, 512:, :], val[va, h], 1, 0) + dot(et[1, 512:, :], val[vb, h], 1, 0)).astype(BF16)
        go(gcopy[i])
        gkeep[i] = dot(et[0, :512, :], val[va, h], 1, 0) + dot(et[1, :512, :], val[vb, h], 1, 0)

    xcopy = {}
    for i in range(8):
        for k in range(3):
            xcopy[i, k] = remote(xs.at[i, k], xr.at[i, k], xssem.at[i, k], xrsem.at[i, k], xdev[k])

    def x_send(f, h):
        i = f * 4 + h
        gcopy[i].wait_recv()
        for k in (1, 0, 2):
            rows = slice((k + 1) * 128, (k + 2) * 128)
            xs[i, k] = (gkeep[i, rows, :] + gr[i, rows, :].astype(F32)).astype(BF16)
            go(xcopy[i, k])

    fcopy, flocal = {}, {}
    for i in range(8):
        where = dev(x, c, m, z, m if i < 4 else 1 - m)
        fcopy[i] = remote(fs.at[i], val_out.at[s, i % 4], fssem.at[i], frsem.at[s, i % 4], where)
        flocal[i] = pltpu.make_async_copy(fs.at[i], val_out.at[s, i % 4], frsem.at[s, i % 4])

    def f_send(f, h):
        i = f * 4 + h
        value = gkeep[i, :128, :] + gr[i, :128, :].astype(F32)
        for k in range(3):
            xcopy[i, k].wait_recv()
            value = value + xr[i, k].astype(F32)
        fs[i] = value.astype(BF16)
        if f == 0:
            @pl.when(selfy)
            def _():
                flocal[i].start()

            @pl.when(jnp.logical_not(selfy))
            def _():
                fcopy[i].start()
        else:
            go(fcopy[i])

    def f_in(h):
        for half in range(2):
            remote(fs.at[h], val_out.at[half, h], fssem.at[h], frsem.at[half, h], n1).wait_recv()

    w_left = [0, 1]

    def value_on(to, i):
        if to == 3 and i < WINDOW:
            j = 0 if i <= WINDOW // 2 else 1
            if j in w_left:
                w_left.remove(j)
                sent(w_in[j])
        value_next(to, i)

    def weights_in():
        for copy in w_c.values():
            copy.wait_recv()

    steps = {
        "et": enc_first, "second": enc_second, "e": enc_in, "v": value_on, "won": weight_on, "wac": weight_across,
        "wdone": weights_in, "zf": z_first, "zs": z_start, "z": z_step, "ze": z_end, "out": lambda: go(out_copy),
        "g": g_head, "x": x_send, "f": f_send, "fin": f_in,
    }
    for what, *which in ORDER:
        steps[what](*which)
    own_copy.start()
    out_copy.wait_recv()
    for copy in sends:
        copy.wait_send()
    for i in range(4):
        @pl.when(jnp.logical_not(selfy))
        def _():
            fcopy[i].wait_send()
    own_copy.wait()


def finish(enc_in, val_in, eg_out, vg_out):
    for half in range(2):
        eg_out[:, half * 128 : (half + 1) * 128] = enc_in[half]
        for h in range(4):
            vg_out[0, half * 128 : (half + 1) * 128, h * 256 : (h + 1) * 256] = val_in[half, h].astype(F32)


def local(enc_states, value_weight, attn_weights, ctx_grad, prompt_lengths):
    anywhere = pl.BlockSpec(memory_space=pl.ANY)
    vmem = pl.BlockSpec(memory_space=pltpu.VMEM)
    dma = pltpu.SemaphoreType.DMA
    enc_halves, value_parts = pl.pallas_call(
        kernel,
        out_shape=(jax.ShapeDtypeStruct((2, 512, 128), BF16), jax.ShapeDtypeStruct((2, 4, 128, 256), BF16)),
        in_specs=[pl.BlockSpec(memory_space=pltpu.SMEM)] + [anywhere] * 4,
        out_specs=(anywhere, anywhere),
        scratch_shapes=[
            pltpu.VMEM((4, 256, 512), BF16),
            pltpu.VMEM((256, 1024), BF16),
            pltpu.VMEM((2, 8, 512, 128), BF16),
            pltpu.VMEM((2, 1024, 512), BF16),
            pltpu.VMEM((4, 4, 512, 256), BF16),
            pltpu.VMEM((2, 1024, 1024), BF16),
            pltpu.VMEM((2, 8, 512, 128), F32),
            pltpu.VMEM((2, 2, 4, 4, 128, 128), BF16),
            pltpu.VMEM((2, 2, 4, 4, 128, 128), BF16),
            pltpu.VMEM((8, 512, 256), F32),
            pltpu.VMEM((8, 512, 256), BF16),
            pltpu.VMEM((8, 512, 256), BF16),
            pltpu.VMEM((8, 3, 128, 256), BF16),
            pltpu.VMEM((8, 3, 128, 256), BF16),
            pltpu.VMEM((8, 128, 256), BF16),
            pltpu.VMEM((2, 512, 128), BF16),
            dma((6,)), dma((8,)),
            dma((2, 8, 2)), dma((2, 8, 2)),
            dma((4, 4, 2)), dma((4, 4, 2)),
            dma((8, 2)), dma((8, 2)),
            dma((2, 2, 4, 4)), dma((2, 2, 4, 4)),
            dma((8,)), dma((8,)),
            dma((8, 3)), dma((8, 3)),
            dma((8,)), dma((2, 4)),
            dma((2,)), dma((1,)),
        ],
        compiler_params=pltpu.CompilerParams(
            collective_id=0, has_side_effects=True, vmem_limit_bytes=60 * 2**20
        ),
        cost_estimate=pl.CostEstimate(flops=9 * 10**9, bytes_accessed=12 * 2**20, transcendentals=0),
    )(prompt_lengths, enc_states, value_weight, attn_weights, ctx_grad)
    return pl.pallas_call(
        finish,
        out_shape=(jax.ShapeDtypeStruct((512, 256), BF16), jax.ShapeDtypeStruct((1, 256, 1024), F32)),
        in_specs=[vmem, vmem],
        out_specs=(vmem, vmem),
    )(enc_halves, value_parts)


def solution(mesh):
    in_specs = (
        P("dp", ("section", "mp")),
        P("section", None, "mp"),
        P("section", "mp", "dp", None),
        P("section", "dp", "mp"),
        P("dp"),
    )
    out_specs = (P("dp", ("section", "mp")), P("section", "dp", "mp"))
    return jax.shard_map(local, mesh=mesh, in_specs=in_specs, out_specs=out_specs, check_vma=False)
```
